32 devices in a mesh: groups: 2 (over y), expert: 8 (over z, core), dp: 2 (over x).
Axes of the slice: x: 2, y: 2, z: 4, core: 2. Of those that a mesh axis runs over, the one named last changes fastest.
Arguments:
- tokens: bfloat16 [240, 2048], P(('groups', 'expert'), 'dp'), parts along dimension 0, may hold values from -6 to 6
- routes: int32 [240, 8], P(('groups', 'expert')), parts along dimension 0, may hold values from 0 to 15, all different within a row; in each aligned block of 15 rows (0 to 14, 15 to 29, ...) at most 11 rows name the same one
- route_weights: float32 [240, 8], P(('groups', 'expert')), parts along dimension 0, may hold values from 0.1 to 0.5
- w_gate: bfloat16 [16, 2048, 768], P('expert', 'dp'), may hold values from -0.125 to 0.125
- w_up: bfloat16 [16, 2048, 768], P('expert', 'dp'), may hold values from -0.125 to 0.125
- w_down: bfloat16 [16, 768, 2048], P('expert', None, 'dp'), may hold values from -0.21875 to 0.21875
- sae_encoder: bfloat16 [2048, 3072], P(None, ('expert', 'dp')), may hold values from -0.25 to 0.25
- enc_bias: float32 [3072], P(('expert', 'dp')), may hold values from -1 to 0.5
- sae_decoder: bfloat16 [3072, 2048], P(('expert', 'dp')), may hold values from -1 to 1
- dec_bias: float32 [2048], replicated, may hold values from -1.2 to 1.2
Outputs:
- moe_out: bfloat16 [240, 2048], P(('groups', 'expert'), 'dp'), parts along dimension 0
- grad_encoder: bfloat16 [4096, 3072], P('groups', ('expert', 'dp')), parts along dimension 0
- grad_decoder: bfloat16 [3072, 4096], P(('expert', 'dp'), 'groups'), parts along dimension 1
- grad_enc_bias: float32 [6144], P(('groups', 'expert', 'dp')), parts along dimension 0
- grad_dec_bias: float32 [4096], P('groups'), parts along dimension 0
- loss_mean: float32 [2], P('groups'), parts along dimension 0
The draws below stay inside these ranges and needn't reach their ends.
There are 2 independent parts, one for each index of `groups`. The reference program is written for one: setup_inputs(seed, part) draws one part's arguments, and reference() takes and returns one part's arrays. A program takes and returns all parts, laid end to end along the dimension named above; an argument that names none is the same for every part. Nothing has to cross between parts.
Inputs may be any that keep to these rules, and one draw needn't show every extreme that they name: `routes`: in each aligned block of 15 rows (the rows of one index of the expert axis), no expert is named by more than 11 rows, and some block has an expert named by exactly 11 rows.
All inputs are finite; a program needn't handle non-finite values.
Results may differ from the reference program's by a relative error of at most 0.0085.
Values may be sent and summed in bfloat16 or wider, within the bound.
A program may use at most 64 MiB of HBM per device.

```python
import math
import jax
import jax.numpy as jnp
import numpy as np
from jax import lax

D = 2048
FF = 768
TOP = 8
TOK_DEV = 15
EXPERTS = 16
CAP = 11
N_TOK = 120
LATENTS = 3072
N_EXPERT = 8


def draw_sae_decoder(key, part):
    key = jax.random.fold_in(key, 11)
    row_key, entry_key = jax.random.split(key)
    scales = jnp.exp(jax.random.uniform(row_key, (LATENTS, 1), jnp.float32, math.log(0.4), math.log(4.0)))
    entries = jnp.clip(jax.random.normal(entry_key, (LATENTS, D), jnp.float32), -4.0, 4.0)
    values = jnp.clip(entries * scales / math.sqrt(LATENTS), -1.0, 1.0)
    return values.astype(jnp.bfloat16)


def level_of(own_key, shape, pieces, low, top_value):
    factor_of = 1.0
    for dim, shards_of in pieces:
        draws = jax.random.uniform(jax.random.fold_in(jax.random.fold_in(own_key, 6), dim), (shards_of,), jnp.float32, low / len(pieces), top_value / len(pieces))
        factor_of = factor_of * jnp.repeat(jnp.exp(draws), shape[dim] // shards_of).reshape((-1,) + (1,) * (len(shape) - 1 - dim))
    return factor_of


def shared_out(own_key, own, number, rows, number_of, top, limit, skew):
    order = jax.random.permutation(own_key, number_of)
    crowded, usual = shares(number_of, rows * top, limit, skew, True), shares(number_of, rows * top, limit, skew, False)
    places = jnp.arange(number_of)

    def named(tallies, offset_by):
        used = int((tallies > 0).sum())
        fixed = max(1, used // 4)
        passed = fixed + (places - fixed + offset_by * (used - fixed)) % max(1, number_of - fixed)
        return jnp.zeros((number_of,), jnp.int32).at[order[jnp.where(places < fixed, places, passed)]].set(jnp.asarray(tallies, jnp.int32))

    tallies = jnp.where(number % 4 == 0, named(crowded, number // 4), named(usual, number - number // 4 - 1))
    mixed = jax.random.permutation(jax.random.fold_in(own, 3), number_of)
    giver, taker = mixed[0:number_of // 2 * 2:2], mixed[1:number_of // 2 * 2:2]
    slack = jnp.minimum(tallies[giver] - 1, limit - tallies[taker]) // 2
    slack = jnp.where((giver == order[0]) | (taker == order[0]) | (tallies[taker] == 0), 0, jnp.maximum(slack, 0))
    passed = jax.random.randint(jax.random.fold_in(own, 4), (number_of // 2,), 0, 1 << 20) % (slack + 1)
    tallies = tallies.at[giver].add(-passed).at[taker].add(passed)
    members = jnp.searchsorted(jnp.cumsum(tallies), jnp.arange(rows * top), side="right").astype(jnp.int32)
    table = members.reshape(top, rows).T
    table = table[jax.random.permutation(jax.random.fold_in(own, 1), rows)]
    offset_by = jax.random.randint(jax.random.fold_in(own, 2), (rows, 1), 0, top)
    return jnp.take_along_axis(table, (jnp.arange(top)[None, :] + offset_by) % top, axis=1)


def shares(amount, total, bound, lean, full):
    portions = [(1 << 20) // math.isqrt(grade ** lean) + 1 for grade in range(1, amount + 1)]
    largest = bound if full else min(bound, max(-(-total // amount), total * portions[0] // sum(portions)))
    least = 1 if total - largest >= amount - 1 else 0
    counts, spare = [largest] + [least] * (amount - 1), total - largest - least * (amount - 1)
    while spare > 0:
        movable = [i for i in range(1, amount) if counts[i] < largest] or [i for i in range(1, amount) if counts[i] < bound]
        mass, budget = sum([portions[i] for i in movable]), spare
        for i in movable:
            more = min(bound - counts[i], max(1, budget * portions[i] // mass), spare)
            counts[i] = counts[i] + more
            spare = spare - more
    return np.array(counts)


def normal_values(own_key, extent, width, limit, cuts=(), held_as=jnp.bfloat16):
    level = level_of(own_key, extent, cuts, -0.22, 0.18) if cuts else 1.0
    values = jax.random.normal(own_key, extent, jnp.float32) * width * level
    return jnp.minimum(jnp.maximum(values, -limit), limit).astype(held_as)


def setup_inputs(seed: int = 0, part: int = 0) -> dict:
    streams_of = jax.random.split(jax.random.key(seed), 11)
    own_keys = jax.random.split(jax.random.fold_in(streams_of[10], part), 11)
    tokens = normal_values(own_keys[0], (N_TOK, D), 1.0, 6.0, ((0, 8), (1, 2)))
    routes_keys = jax.random.split(jax.random.fold_in(own_keys[1], 1), N_TOK // TOK_DEV)
    routes_turns = jax.random.permutation(jax.random.fold_in(own_keys[1], 3), N_TOK // TOK_DEV)
    routes = jax.vmap(lambda own, number: shared_out(jax.random.fold_in(own_keys[1], 2), own, number, TOK_DEV, EXPERTS, TOP, CAP, 2))(routes_keys, routes_turns).reshape((N_TOK, TOP))
    route_weights = jnp.clip(0.1 + 0.4 * jax.random.uniform(own_keys[2], (N_TOK, TOP), jnp.float32) ** level_of(own_keys[2], (N_TOK, TOP), ((0, 8),), -0.2, 0.2), 0.1, 0.5)
    w_gate = normal_values(streams_of[3], (EXPERTS, D, FF), D ** -0.5, 0.125, ((0, 8), (1, 2)))
    w_up = normal_values(streams_of[4], (EXPERTS, D, FF), D ** -0.5, 0.125, ((0, 8), (1, 2)))
    w_down = normal_values(streams_of[5], (EXPERTS, FF, D), FF ** -0.5, 0.21875, ((0, 8), (2, 2)))
    sae_encoder = normal_values(streams_of[6], (D, LATENTS), (D // 4) ** -0.5, 0.25, ((1, 16),))
    enc_bias = jnp.clip(-1.0 + 1.5 * jax.random.uniform(streams_of[7], (LATENTS,), jnp.float32) ** level_of(streams_of[7], (LATENTS,), ((0, 16),), -0.2, 0.2), -1.0, 0.5)
    sae_decoder = draw_sae_decoder(jax.random.fold_in(streams_of[10], 71), part)
    dec_bias = normal_values(streams_of[9], (D,), 0.3, 1.2, (), jnp.float32)
    return {"tokens": tokens, "routes": routes, "route_weights": route_weights, "w_gate": w_gate, "w_up": w_up, "w_down": w_down, "sae_encoder": sae_encoder, "enc_bias": enc_bias, "sae_decoder": sae_decoder, "dec_bias": dec_bias}


PENALTY = 0.5
SHARPNESS = 4.0
EPSILON = 1e-06

def run_expert(operands):
    slot_rows, gate_mat, up_mat, down_mat = operands
    gate_pre = jnp.dot(slot_rows, gate_mat, preferred_element_type=jnp.float32)
    up_pre = jnp.dot(slot_rows, up_mat, preferred_element_type=jnp.float32)
    hidden = (jax.nn.silu(gate_pre) * up_pre).astype(jnp.bfloat16)
    return jnp.dot(hidden, down_mat, preferred_element_type=jnp.float32).astype(jnp.bfloat16)

def reference(tokens, routes, route_weights, w_gate, w_up, w_down, sae_encoder, enc_bias, sae_decoder, dec_bias):
    per_expert = N_EXPERT * CAP
    flat_routes = routes.reshape(-1).astype(jnp.int32)
    expert_hot = (flat_routes[:, None] == jnp.arange(EXPERTS, dtype=jnp.int32)[None, :]).astype(jnp.int32)
    earlier = jnp.cumsum(expert_hot, axis=0) - expert_hot
    position = lax.optimization_barrier(jnp.sum(earlier * expert_hot, axis=1)).astype(jnp.int32)
    slot_index = (flat_routes * per_expert + position).astype(jnp.int32)
    token_rows = jnp.repeat(tokens, TOP, axis=0)
    buffers = jnp.zeros((EXPERTS * per_expert, D), tokens.dtype).at[slot_index].set(token_rows)
    buffers = buffers.reshape(EXPERTS, per_expert, D)
    outputs = lax.map(run_expert, (buffers, w_gate, w_up, w_down))
    slot_out = outputs.reshape(EXPERTS * per_expert, D)[slot_index].astype(jnp.float32).reshape(N_TOK, TOP, D)
    combined = lax.optimization_barrier(jnp.sum(slot_out * route_weights[:, :, None], axis=1))
    moe_out = combined.astype(jnp.bfloat16)
    centered = (moe_out.astype(jnp.float32) - dec_bias).astype(jnp.bfloat16)
    pre_act = jnp.dot(centered, sae_encoder, preferred_element_type=jnp.float32) + enc_bias
    latent_codes = jax.nn.softplus(SHARPNESS * pre_act) / SHARPNESS
    codes_b = latent_codes.astype(jnp.bfloat16)
    decoder_wide = sae_decoder.astype(jnp.float32)
    dec_norm = jnp.sqrt(lax.optimization_barrier(jnp.sum(decoder_wide * decoder_wide, axis=1)) + EPSILON)
    recon = jnp.dot(codes_b, sae_decoder, preferred_element_type=jnp.float32) + dec_bias
    residual = recon - moe_out.astype(jnp.float32)
    d_recon = (2.0 * residual).astype(jnp.bfloat16)
    grad_codes = jnp.dot(d_recon, sae_decoder.T, preferred_element_type=jnp.float32) + PENALTY * dec_norm
    d_pre = grad_codes * jax.nn.sigmoid(SHARPNESS * pre_act)
    d_pre_b = d_pre.astype(jnp.bfloat16)
    grad_encoder = jnp.dot(centered.T, d_pre_b, preferred_element_type=jnp.float32).astype(jnp.bfloat16)
    code_totals = lax.optimization_barrier(jnp.sum(latent_codes, axis=0))
    grad_decoder = jnp.dot(codes_b.T, d_recon, preferred_element_type=jnp.float32)
    grad_decoder = grad_decoder + PENALTY * code_totals[:, None] * decoder_wide / dec_norm[:, None]
    grad_decoder = grad_decoder.astype(jnp.bfloat16)
    grad_enc_bias = lax.optimization_barrier(jnp.sum(d_pre, axis=0))
    pre_totals = lax.optimization_barrier(jnp.sum(d_pre_b.astype(jnp.float32), axis=0))
    bias_pull = jnp.dot(sae_encoder.astype(jnp.float32), pre_totals, precision=lax.Precision.HIGHEST)
    grad_dec_bias = lax.optimization_barrier(jnp.sum(d_recon.astype(jnp.float32), axis=0)) - bias_pull
    objective = jnp.sum(residual * residual) + PENALTY * jnp.sum(latent_codes * dec_norm)
    loss_mean = (objective / (N_TOK * D)).reshape(1)
    return (moe_out, grad_encoder, grad_decoder, grad_enc_bias, grad_dec_bias, loss_mean)
```

```python
import functools

import jax
import jax.numpy as jnp
from jax import lax
from jax.experimental import pallas as pl
from jax.experimental.pallas import tpu as pltpu
from jax.sharding import PartitionSpec as P

PENALTY = 0.5
SHARPNESS = 4.0
EPSILON = 1e-06


def gather_tokens(local_block):
    widened = lax.all_gather(local_block, "dp", axis=1, tiled=True)
    return lax.all_gather(widened, "expert", axis=0, tiled=True)


def local_plain(
    tokens,
    routes,
    route_weights,
    w_gate,
    w_up,
    w_down,
    sae_encoder,
    enc_bias,
    sae_decoder,
    dec_bias,
):
    tok_count, top_count = routes.shape
    feature_width = tokens.shape[1]
    local_experts = w_gate.shape[0]
    peer_count = lax.axis_size("expert")
    total_experts = local_experts * peer_count
    capacity = min(tok_count, max(2, tok_count * top_count * 3 // (2 * total_experts)))
    flat_routes = routes.reshape(-1)
    expert_hot = (
        flat_routes[:, None] == jnp.arange(total_experts, dtype=jnp.int32)[None, :]
    ).astype(jnp.int32)
    earlier = jnp.cumsum(expert_hot, axis=0) - expert_hot
    position = jnp.sum(earlier * expert_hot, axis=1)
    slot_index = flat_routes * capacity + position
    slot_hot = slot_index[:, None] == jnp.arange(total_experts * capacity, dtype=jnp.int32)[None, :]
    slot_hot = slot_hot.reshape(tok_count, top_count, total_experts * capacity)
    dispatch_map = jnp.sum(slot_hot.astype(jnp.int32), axis=1).astype(jnp.bfloat16)
    combine_map = jnp.sum(slot_hot.astype(jnp.float32) * route_weights[:, :, None], axis=1)
    send_rows = lax.dot_general(
        dispatch_map, tokens, (((0,), (0,)), ((), ())), preferred_element_type=jnp.float32
    )
    send_blocks = send_rows.astype(jnp.bfloat16).reshape(
        peer_count, local_experts, capacity, feature_width
    )
    received = lax.all_to_all(send_blocks, "expert", split_axis=0, concat_axis=0, tiled=True)
    gate_part = jnp.einsum("secd,edf->secf", received, w_gate, preferred_element_type=jnp.float32)
    up_part = jnp.einsum("secd,edf->secf", received, w_up, preferred_element_type=jnp.float32)
    gate_full, up_full = lax.psum((gate_part, up_part), "dp")
    hidden = (jax.nn.silu(gate_full) * up_full).astype(jnp.bfloat16)
    outputs = jnp.einsum("secf,efd->secd", hidden, w_down, preferred_element_type=jnp.float32)
    returned = lax.all_to_all(
        outputs.astype(jnp.bfloat16), "expert", split_axis=0, concat_axis=0, tiled=True
    )
    returned_rows = returned.reshape(total_experts * capacity, feature_width).astype(jnp.float32)
    combined = jnp.dot(combine_map, returned_rows, precision=lax.Precision.HIGHEST)
    moe_out = combined.astype(jnp.bfloat16)
    all_tokens = gather_tokens(moe_out)
    centered = (all_tokens.astype(jnp.float32) - dec_bias).astype(jnp.bfloat16)
    pre_act = jnp.dot(centered, sae_encoder, preferred_element_type=jnp.float32) + enc_bias
    latent_codes = jax.nn.softplus(SHARPNESS * pre_act) / SHARPNESS
    codes_b = latent_codes.astype(jnp.bfloat16)
    decoder_wide = sae_decoder.astype(jnp.float32)
    dec_norm = jnp.sqrt(jnp.sum(decoder_wide * decoder_wide, axis=1) + EPSILON)
    partial_rows = lax.psum_scatter(
        jnp.dot(codes_b, sae_decoder, preferred_element_type=jnp.float32).astype(jnp.bfloat16),
        "expert",
        scatter_dimension=0,
        tiled=True,
    )
    recon_share = lax.psum_scatter(partial_rows, "dp", scatter_dimension=1, tiled=True).astype(
        jnp.float32
    )
    bias_share = lax.dynamic_slice_in_dim(
        dec_bias, lax.axis_index("dp") * feature_width, feature_width, 0
    )
    residual = recon_share + bias_share - moe_out.astype(jnp.float32)
    d_recon_share = (2.0 * residual).astype(jnp.bfloat16)
    d_recon = gather_tokens(d_recon_share)
    grad_codes = lax.dot_general(
        d_recon, sae_decoder, (((1,), (1,)), ((), ())), preferred_element_type=jnp.float32
    )
    d_pre = (grad_codes + PENALTY * dec_norm) * jax.nn.sigmoid(SHARPNESS * pre_act)
    d_pre_b = d_pre.astype(jnp.bfloat16)
    grad_encoder = lax.dot_general(
        centered, d_pre_b, (((0,), (0,)), ((), ())), preferred_element_type=jnp.float32
    )
    code_totals = jnp.sum(latent_codes, axis=0)
    grad_decoder = lax.dot_general(
        codes_b, d_recon, (((0,), (0,)), ((), ())), preferred_element_type=jnp.float32
    )
    grad_decoder = grad_decoder + PENALTY * code_totals[:, None] * decoder_wide / dec_norm[:, None]
    grad_enc_bias = jnp.sum(d_pre, axis=0)
    pre_totals = jnp.sum(d_pre_b.astype(jnp.float32), axis=0)
    bias_pull = jnp.dot(
        sae_encoder.astype(jnp.float32), pre_totals, precision=lax.Precision.HIGHEST
    )
    objective_part = jnp.sum(residual * residual) + PENALTY * jnp.sum(latent_codes * dec_norm)
    pull_total, objective = lax.psum((bias_pull, objective_part), ("expert", "dp"))
    grad_dec_bias = jnp.sum(d_recon.astype(jnp.float32), axis=0) - pull_total
    token_total = d_recon.shape[0]
    loss_mean = (objective / (token_total * d_recon.shape[1])).reshape(1)
    return (
        moe_out,
        grad_encoder.astype(jnp.bfloat16),
        grad_decoder.astype(jnp.bfloat16),
        grad_enc_bias,
        grad_dec_bias,
        loss_mean,
    )


ROWS = 16
NT = (((1,), (1,)), ((), ()))
F32 = jnp.float32
BF16 = jnp.bfloat16
MESH_IDS = pl.DeviceIdType.MESH


def mm(a, b):
    return jnp.dot(a, b, preferred_element_type=F32)


def layer_kernel(
    n_tok,
    n_chip,
    tokens,
    routes,
    route_weights,
    w_gate,
    w_up,
    w_down,
    enc_hbm,
    enc_bias,
    dec_hbm,
    dec_bias,
    moe_out,
    g_enc,
    g_dec,
    g_enc_bias,
    g_dec_bias,
    loss,
    wg,
    wu,
    wd,
    enc,
    dec,
    tok_all,
    weight_all,
    part_send,
    part_recv,
    own_pre,
    hid_send,
    hid_recv,
    moe_sib_send,
    moe_sib_recv,
    moe_own,
    moe_z_send,
    moe_z_recv,
    moe_all,
    rec_sib_send,
    rec_sib_recv,
    rec_own,
    rec_dp_send,
    rec_dp_recv,
    rec_z_send,
    rec_z_recv,
    d_all,
    tot_send,
    tot_recv,
    centered_t,
    load_sem,
    send_sem,
    tok_sem,
    weight_sem,
    pair_sem,
    moe_sem,
    moe_all_sem,
    rec_sem,
    d_all_sem,
    tot_sem,
):
    expert = lax.axis_index("expert")
    p = lax.axis_index("dp")
    z, c = expert // 2, expert % 2
    q, s = 1 - p, 1 - c
    half = tokens.shape[1]
    width = 2 * half
    ff = wg.shape[2]
    rows = 2 * n_chip * ROWS
    side = n_chip * ROWS

    loads = []
    for slot, (hbm, vmem) in enumerate(
        (
            (w_gate.at[q], wg.at[0]),
            (w_up.at[q], wu.at[0]),
            (w_gate.at[p], wg.at[1]),
            (w_up.at[p], wu.at[1]),
            (w_down.at[p], wd.at[1]),
            (w_down.at[q], wd.at[0]),
            (dec_hbm, dec),
            (enc_hbm, enc),
        )
    ):
        load = pltpu.make_async_copy(hbm, vmem, load_sem.at[slot])
        load.start()
        loads.append(load)

    sibling = {"expert": z * 2 + s, "dp": p}
    across = {"expert": expert, "dp": q}
    chips = [{"expert": lax.rem(z + d, n_chip) * 2 + c, "dp": p} for d in range(n_chip)]

    barrier = pltpu.get_barrier_semaphore()
    peers = [sibling, across] + chips[1:]
    for peer in peers:
        pl.semaphore_signal(barrier, inc=1, device_id=peer, device_id_type=MESH_IDS)

    base = pl.multiple_of((c * n_chip + z) * ROWS, ROWS)
    block = jnp.concatenate(
        [tokens[...], jnp.zeros((ROWS - n_tok, half), BF16)], axis=0
    )
    tok_all[pl.ds(base, ROWS), :] = block
    lane = lax.broadcasted_iota(jnp.int32, (n_tok, 128), 1)
    dense = jnp.zeros((n_tok, 128), F32)
    for k in range(routes.shape[1]):
        dense += jnp.where(lane == routes[:, k : k + 1], route_weights[:, k : k + 1], 0.0)
    weight_all[pl.ds(base, ROWS), :] = jnp.concatenate(
        [dense, jnp.zeros((ROWS - n_tok, 128), F32)], axis=0
    )
    pl.semaphore_wait(barrier, len(peers))

    pending = []

    def send(src, dst, recv, device):
        copy = pltpu.make_async_remote_copy(
            src_ref=src,
            dst_ref=dst,
            send_sem=send_sem.at[len(pending)],
            recv_sem=recv,
            device_id=device,
            device_id_type=MESH_IDS,
        )
        copy.start()
        pending.append(copy)

    def arrived(dst, recv):
        pltpu.make_async_remote_copy(
            src_ref=dst,
            dst_ref=dst,
            send_sem=send_sem.at[0],
            recv_sem=recv,
            device_id=across,
            device_id_type=MESH_IDS,
        ).wait_recv()

    def row_of(zz, cc):
        return pl.multiple_of((cc * n_chip + zz) * ROWS, ROWS)

    near = [lax.rem(z - d + n_chip, n_chip) for d in range(n_chip)]

    def rows_block(ref, zz, cc):
        return ref.at[pl.ds(row_of(zz, cc), ROWS), :]

    def gather_rows(pairs):
        for d in range(1, n_chip):
            for ref, sem in pairs:
                blk = rows_block(ref, z, c)
                send(blk, blk, sem.at[c * n_chip + z], chips[d])
        for d in range(n_chip):
            for ref, sem in pairs:
                blk = rows_block(ref, near[d], c)
                at = sem.at[c * n_chip + near[d]]
                if d:
                    arrived(blk, at)
                send(blk, blk, at, sibling)

    def finish_rows(ref, sem):
        for d in range(n_chip):
            arrived(rows_block(ref, near[d], s), sem.at[s * n_chip + near[d]])

    gather_rows([(tok_all, tok_sem), (weight_all, weight_sem)])

    loads[6].wait()
    squares = dec[...].astype(F32)
    norm_col = jnp.sqrt(jnp.sum(squares * squares, axis=1, keepdims=True) + EPSILON)
    latents = norm_col.shape[0]
    norm_rows = jnp.broadcast_to(norm_col, (latents, 128)).T
    norm_row = norm_rows[0:1, :]

    finish_rows(tok_all, tok_sem)

    tile = 256
    for which, weights in enumerate((wg, wu)):
        loads[which].wait()
        for at in range(0, ff, tile):
            part_send[which, :, at : at + tile] = mm(
                tok_all[...], weights[0, :, at : at + tile]
            ).astype(BF16)
        send(part_send.at[which], part_recv.at[which], pair_sem.at[which], across)
    for which, weights in enumerate((wg, wu)):
        loads[2 + which].wait()
        for at in range(0, ff, tile):
            own_pre[which, :, at : at + tile] = mm(tok_all[...], weights[1, :, at : at + tile])
    arrived(part_recv.at[0], pair_sem.at[0])
    gate = own_pre[0] + part_recv[0].astype(F32)
    gate = gate / (1.0 + jnp.exp(-gate))
    arrived(part_recv.at[1], pair_sem.at[1])
    hid_send[...] = (gate * (own_pre[1] + part_recv[1].astype(F32))).astype(BF16)
    send(hid_send, hid_recv, pair_sem.at[2], across)

    finish_rows(weight_all, weight_sem)
    lane_all = lax.broadcasted_iota(jnp.int32, (rows, 128), 1)

    def share_of(index):
        return jnp.sum(
            jnp.where(lane_all == expert * 2 + index, weight_all[...], 0.0), axis=1, keepdims=True
        )

    share_own, share_other = share_of(p), share_of(q)
    loads[4].wait()
    moe_own[...] = share_own * mm(hid_send[...], wd[1])
    loads[5].wait()
    arrived(hid_recv, pair_sem.at[2])
    sib_at = pl.multiple_of(s * side, side)
    own_at = pl.multiple_of(c * side, side)
    moe_own[...] += share_other * mm(hid_recv[...], wd[0])

    moe_sib_send[...] = moe_own[pl.ds(sib_at, side), :].astype(BF16)
    send(moe_sib_send, moe_sib_recv, moe_sem.at[n_chip], sibling)
    arrived(moe_sib_recv, moe_sem.at[n_chip])
    for d in list(range(1, n_chip)) + [0]:
        zz = lax.rem(z + d, n_chip)
        own_rows = pl.ds(pl.multiple_of(zz * ROWS, ROWS), ROWS)
        total = moe_own[pl.ds(row_of(zz, c), ROWS), :] + moe_sib_recv[own_rows, :].astype(F32)
        if d:
            moe_z_send[d] = total.astype(BF16)
            send(moe_z_send.at[d], moe_z_recv.at[d], moe_sem.at[d], chips[d])
    for d in range(1, n_chip):
        arrived(moe_z_recv.at[d], moe_sem.at[d])
        total += moe_z_recv[d].astype(F32)
    moe_block = total.astype(BF16)
    moe_out[...] = moe_block[:n_tok]
    own_cols = pl.ds(pl.multiple_of(p * half, half), half)
    other_cols = pl.ds(pl.multiple_of(q * half, half), half)
    moe_all[pl.ds(base, ROWS), own_cols] = moe_block

    def gather_all(ref, sem):
        def blk(zz, cc, cols):
            return ref.at[pl.ds(row_of(zz, cc), ROWS), cols]

        def at(zz, cc, pp):
            return sem.at[(cc * n_chip + zz) * 2 + pp]

        for d in range(1, n_chip):
            send(blk(z, c, own_cols), blk(z, c, own_cols), at(z, c, p), chips[d])
        for zz in near:
            if zz is not near[0]:
                arrived(blk(zz, c, own_cols), at(zz, c, p))
            send(blk(zz, c, own_cols), blk(zz, c, own_cols), at(zz, c, p), across)
            send(blk(zz, c, own_cols), blk(zz, c, own_cols), at(zz, c, p), sibling)
        for zz in near:
            arrived(blk(zz, c, other_cols), at(zz, c, q))
            send(blk(zz, c, other_cols), blk(zz, c, other_cols), at(zz, c, q), sibling)
        for zz in near:
            arrived(blk(zz, s, own_cols), at(zz, s, p))
            arrived(blk(zz, s, other_cols), at(zz, s, q))

    gather_all(moe_all, moe_all_sem)
    loads[7].wait()
    centered = (moe_all[...].astype(F32) - dec_bias[...]).astype(BF16)
    pre_act = mm(centered, enc[...]) + enc_bias[...]
    real = lax.broadcasted_iota(jnp.int32, (rows, 1), 0) % ROWS < n_tok
    scaled = SHARPNESS * pre_act
    codes = (jnp.maximum(scaled, 0.0) + jnp.log1p(jnp.exp(-jnp.abs(scaled)))) / SHARPNESS
    codes = jnp.where(real, codes, 0.0)
    codes_b = codes.astype(BF16)

    rec_own[...] = mm(codes_b, dec[...])
    rec_sib_send[...] = rec_own[pl.ds(sib_at, side), :].astype(BF16)
    send(rec_sib_send, rec_sib_recv, rec_sem.at[0], sibling)
    gates = 1.0 / (1.0 + jnp.exp(-scaled))
    gates = jnp.where(real, gates, 0.0)
    arrived(rec_sib_recv, rec_sem.at[0])
    order = list(range(1, n_chip)) + [0]
    kept = []
    for d in order:
        zz = lax.rem(z + d, n_chip)
        here = pl.ds(pl.multiple_of(zz * ROWS, ROWS), ROWS)
        there = pl.ds(row_of(zz, c), ROWS)
        rec_dp_send[d] = (
            rec_own[there, other_cols] + rec_sib_recv[here, other_cols].astype(F32)
        ).astype(BF16)
        send(rec_dp_send.at[d], rec_dp_recv.at[d], rec_sem.at[1 + d], across)
        kept.append(rec_own[there, own_cols] + rec_sib_recv[here, own_cols].astype(F32))
    for d, part in zip(order, kept):
        arrived(rec_dp_recv.at[d], rec_sem.at[1 + d])
        recon = part + rec_dp_recv[d].astype(F32)
        if d:
            rec_z_send[d] = recon.astype(BF16)
            send(rec_z_send.at[d], rec_z_recv.at[d], rec_sem.at[1 + n_chip + d], chips[d])
    centered_t[...] = centered.T
    codes_t = codes.T
    code_totals = jnp.sum(codes_t, axis=1, keepdims=True)
    codes_bt = codes_t.astype(BF16)
    pull_scale = PENALTY * code_totals / norm_col
    for d in range(1, n_chip):
        arrived(rec_z_recv.at[d], rec_sem.at[1 + n_chip + d])
        recon += rec_z_recv[d].astype(F32)
    residual = recon + dec_bias[:, own_cols] - moe_all[pl.ds(base, ROWS), own_cols].astype(F32)
    mine = lax.broadcasted_iota(jnp.int32, (ROWS, 1), 0) < n_tok
    residual = jnp.where(mine, residual, 0.0)
    d_all[pl.ds(base, ROWS), own_cols] = (2.0 * residual).astype(BF16)
    objective = jnp.sum(residual * residual) + PENALTY * jnp.sum(codes * norm_row)
    gather_all(d_all, d_all_sem)

    d_recon = d_all[...]
    grad_codes = lax.dot_general(d_recon, dec[...], NT, preferred_element_type=F32)
    d_pre = (grad_codes + PENALTY * norm_row) * gates
    d_pre_b = d_pre.astype(BF16)
    g_enc_bias[...] = jnp.sum(d_pre, axis=0, keepdims=True)
    totals = jnp.sum(d_pre_b.astype(F32), axis=0, keepdims=True)
    high = totals.astype(BF16)
    rest = totals - high.astype(F32)
    mid = rest.astype(BF16)
    low = (rest - mid.astype(F32)).astype(BF16)
    thirds = jnp.concatenate(
        [high, mid, low, jnp.zeros((ROWS - 3, latents), BF16)], axis=0
    )
    pulls = lax.dot_general(thirds, enc[...], NT, preferred_element_type=F32)
    tot_send[0, :, :width] = jnp.sum(pulls, axis=0, keepdims=True)
    tot_send[0, :, width:] = jnp.full((1, 128), objective, F32)

    send(tot_send.at[0], tot_recv.at[0], tot_sem.at[0], sibling)
    mid_at = width // 2
    g_enc[:mid_at, :] = mm(centered_t[:mid_at, :], d_pre_b).astype(BF16)
    arrived(tot_recv.at[0], tot_sem.at[0])
    tot_send[1] = tot_send[0] + tot_recv[0]
    send(tot_send.at[1], tot_recv.at[1], tot_sem.at[1], across)
    g_enc[mid_at:, :] = mm(centered_t[mid_at:, :], d_pre_b).astype(BF16)
    arrived(tot_recv.at[1], tot_sem.at[1])
    tot_send[2] = tot_send[1] + tot_recv[1]
    for d in range(1, n_chip):
        send(tot_send.at[2], tot_recv.at[1 + d], tot_sem.at[1 + d], chips[d])
    g_dec[...] = (mm(codes_bt, d_recon) + pull_scale * dec[...].astype(F32)).astype(BF16)
    d_sum = jnp.sum(d_recon.astype(F32), axis=0, keepdims=True)
    final = tot_send[2]
    for d in range(1, n_chip):
        arrived(tot_recv.at[1 + d], tot_sem.at[1 + d])
        final = final + tot_recv[1 + d]
    g_dec_bias[...] = d_sum - final[:, :width]
    loss[...] = final[:, width:] / (n_tok * 2 * n_chip * width)
    for copy in pending:
        copy.wait_send()


def local_fused(
    tokens,
    routes,
    route_weights,
    w_gate,
    w_up,
    w_down,
    sae_encoder,
    enc_bias,
    sae_decoder,
    dec_bias,
):
    n_tok, half = tokens.shape
    n_chip = lax.axis_size("expert") // 2
    width = 2 * half
    ff = w_gate.shape[2]
    latents = enc_bias.shape[0]
    side = n_chip * ROWS
    rows = 2 * side
    vmem = pl.BlockSpec(memory_space=pltpu.VMEM)
    hbm = pl.BlockSpec(memory_space=pl.ANY)
    dma = pltpu.SemaphoreType.DMA
    scratch = [
        pltpu.VMEM((2, half, ff), BF16),
        pltpu.VMEM((2, half, ff), BF16),
        pltpu.VMEM((2, ff, half), BF16),
        pltpu.VMEM((width, latents), BF16),
        pltpu.VMEM((latents, width), BF16),
        pltpu.VMEM((rows, half), BF16),
        pltpu.VMEM((rows, 128), F32),
        pltpu.VMEM((2, rows, ff), BF16),
        pltpu.VMEM((2, rows, ff), BF16),
        pltpu.VMEM((2, rows, ff), F32),
        pltpu.VMEM((rows, ff), BF16),
        pltpu.VMEM((rows, ff), BF16),
        pltpu.VMEM((side, half), BF16),
        pltpu.VMEM((side, half), BF16),
        pltpu.VMEM((rows, half), F32),
        pltpu.VMEM((n_chip, ROWS, half), BF16),
        pltpu.VMEM((n_chip, ROWS, half), BF16),
        pltpu.VMEM((rows, width), BF16),
        pltpu.VMEM((side, width), BF16),
        pltpu.VMEM((side, width), BF16),
        pltpu.VMEM((rows, width), F32),
        pltpu.VMEM((n_chip, ROWS, half), BF16),
        pltpu.VMEM((n_chip, ROWS, half), BF16),
        pltpu.VMEM((n_chip, ROWS, half), BF16),
        pltpu.VMEM((n_chip, ROWS, half), BF16),
        pltpu.VMEM((rows, width), BF16),
        pltpu.VMEM((3, 1, width + 128), F32),
        pltpu.VMEM((1 + n_chip, 1, width + 128), F32),
        pltpu.VMEM((width, rows), BF16),
        dma((8,)),
        dma((16 * n_chip,)),
        dma((2 * n_chip,)),
        dma((2 * n_chip,)),
        dma((3,)),
        dma((n_chip + 1,)),
        dma((4 * n_chip,)),
        dma((1 + 2 * n_chip,)),
        dma((4 * n_chip,)),
        dma((1 + n_chip,)),
    ]
    outs = pl.pallas_call(
        functools.partial(layer_kernel, n_tok, n_chip),
        out_shape=(
            jax.ShapeDtypeStruct((n_tok, half), BF16),
            jax.ShapeDtypeStruct((width, latents), BF16),
            jax.ShapeDtypeStruct((latents, width), BF16),
            jax.ShapeDtypeStruct((1, latents), F32),
            jax.ShapeDtypeStruct((1, width), F32),
            jax.ShapeDtypeStruct((1, 128), F32),
        ),
        in_specs=[vmem, vmem, vmem, hbm, hbm, hbm, hbm, vmem, hbm, vmem],
        out_specs=(vmem,) * 6,
        scratch_shapes=scratch,
        compiler_params=pltpu.CompilerParams(
            collective_id=0, has_side_effects=True, vmem_limit_bytes=48 * 1024 * 1024
        ),
    )(
        tokens,
        routes,
        route_weights,
        w_gate,
        w_up,
        w_down,
        sae_encoder,
        enc_bias.reshape(1, -1),
        sae_decoder,
        dec_bias.reshape(1, -1),
    )
    moe_out, g_enc, g_dec, g_enc_bias, g_dec_bias, loss = outs
    return moe_out, g_enc, g_dec, g_enc_bias.reshape(-1), g_dec_bias.reshape(-1), loss[0, :1]


def local(*args):
    tokens, w_gate = args[0], args[3]
    pairs = lax.axis_size("dp") == 2 and w_gate.shape[0] == 2
    total_experts = 2 * lax.axis_size("expert")
    if pairs and lax.axis_size("expert") % 2 == 0 and total_experts <= 32 and tokens.shape[0] <= ROWS:
        return local_fused(*args)
    return local_plain(*args)


def solution(mesh):
    in_specs = (
        P(("groups", "expert"), "dp"),
        P(("groups", "expert"), None),
        P(("groups", "expert"), None),
        P("expert", "dp", None),
        P("expert", "dp", None),
        P("expert", None, "dp"),
        P(None, ("expert", "dp")),
        P(("expert", "dp")),
        P(("expert", "dp"), None),
        P(),
    )
    out_specs = (
        P(("groups", "expert"), "dp"),
        P("groups", ("expert", "dp")),
        P(("expert", "dp"), "groups"),
        P(("groups", "expert", "dp")),
        P("groups"),
        P("groups"),
    )
    return jax.shard_map(local, mesh=mesh, in_specs=in_specs, out_specs=out_specs, check_vma=False)
```

```python
import functools

import jax
import jax.numpy as jnp
from jax import lax
from jax.experimental import pallas as pl
from jax.experimental.pallas import tpu as pltpu
from jax.sharding import PartitionSpec as P

PENALTY = 0.5
SHARPNESS = 4.0
EPSILON = 1e-06


def gather_tokens(local_block):
    widened = lax.all_gather(local_block, "dp", axis=1, tiled=True)
    return lax.all_gather(widened, "expert", axis=0, tiled=True)


def local_plain(
    tokens,
    routes,
    route_weights,
    w_gate,
    w_up,
    w_down,
    sae_encoder,
    enc_bias,
    sae_decoder,
    dec_bias,
):
    tok_count, top_count = routes.shape
    feature_width = tokens.shape[1]
    local_experts = w_gate.shape[0]
    peer_count = lax.axis_size("expert")
    total_experts = local_experts * peer_count
    capacity = min(tok_count, max(2, tok_count * top_count * 3 // (2 * total_experts)))
    flat_routes = routes.reshape(-1)
    expert_hot = (
        flat_routes[:, None] == jnp.arange(total_experts, dtype=jnp.int32)[None, :]
    ).astype(jnp.int32)
    earlier = jnp.cumsum(expert_hot, axis=0) - expert_hot
    position = jnp.sum(earlier * expert_hot, axis=1)
    slot_index = flat_routes * capacity + position
    slot_hot = slot_index[:, None] == jnp.arange(total_experts * capacity, dtype=jnp.int32)[None, :]
    slot_hot = slot_hot.reshape(tok_count, top_count, total_experts * capacity)
    dispatch_map = jnp.sum(slot_hot.astype(jnp.int32), axis=1).astype(jnp.bfloat16)
    combine_map = jnp.sum(slot_hot.astype(jnp.float32) * route_weights[:, :, None], axis=1)
    send_rows = lax.dot_general(
        dispatch_map, tokens, (((0,), (0,)), ((), ())), preferred_element_type=jnp.float32
    )
    send_blocks = send_rows.astype(jnp.bfloat16).reshape(
        peer_count, local_experts, capacity, feature_width
    )
    received = lax.all_to_all(send_blocks, "expert", split_axis=0, concat_axis=0, tiled=True)
    gate_part = jnp.einsum("secd,edf->secf", received, w_gate, preferred_element_type=jnp.float32)
    up_part = jnp.einsum("secd,edf->secf", received, w_up, preferred_element_type=jnp.float32)
    gate_full, up_full = lax.psum((gate_part, up_part), "dp")
    hidden = (jax.nn.silu(gate_full) * up_full).astype(jnp.bfloat16)
    outputs = jnp.einsum("secf,efd->secd", hidden, w_down, preferred_element_type=jnp.float32)
    returned = lax.all_to_all(
        outputs.astype(jnp.bfloat16), "expert", split_axis=0, concat_axis=0, tiled=True
    )
    returned_rows = returned.reshape(total_experts * capacity, feature_width).astype(jnp.float32)
    combined = jnp.dot(combine_map, returned_rows, precision=lax.Precision.HIGHEST)
    moe_out = combined.astype(jnp.bfloat16)
    all_tokens = gather_tokens(moe_out)
    centered = (all_tokens.astype(jnp.float32) - dec_bias).astype(jnp.bfloat16)
    pre_act = jnp.dot(centered, sae_encoder, preferred_element_type=jnp.float32) + enc_bias
    latent_codes = jax.nn.softplus(SHARPNESS * pre_act) / SHARPNESS
    codes_b = latent_codes.astype(jnp.bfloat16)
    decoder_wide = sae_decoder.astype(jnp.float32)
    dec_norm = jnp.sqrt(jnp.sum(decoder_wide * decoder_wide, axis=1) + EPSILON)
    partial_rows = lax.psum_scatter(
        jnp.dot(codes_b, sae_decoder, preferred_element_type=jnp.float32).astype(jnp.bfloat16),
        "expert",
        scatter_dimension=0,
        tiled=True,
    )
    recon_share = lax.psum_scatter(partial_rows, "dp", scatter_dimension=1, tiled=True).astype(
        jnp.float32
    )
    bias_share = lax.dynamic_slice_in_dim(
        dec_bias, lax.axis_index("dp") * feature_width, feature_width, 0
    )
    residual = recon_share + bias_share - moe_out.astype(jnp.float32)
    d_recon_share = (2.0 * residual).astype(jnp.bfloat16)
    d_recon = gather_tokens(d_recon_share)
    grad_codes = lax.dot_general(
        d_recon, sae_decoder, (((1,), (1,)), ((), ())), preferred_element_type=jnp.float32
    )
    d_pre = (grad_codes + PENALTY * dec_norm) * jax.nn.sigmoid(SHARPNESS * pre_act)
    d_pre_b = d_pre.astype(jnp.bfloat16)
    grad_encoder = lax.dot_general(
        centered, d_pre_b, (((0,), (0,)), ((), ())), preferred_element_type=jnp.float32
    )
    code_totals = jnp.sum(latent_codes, axis=0)
    grad_decoder = lax.dot_general(
        codes_b, d_recon, (((0,), (0,)), ((), ())), preferred_element_type=jnp.float32
    )
    grad_decoder = grad_decoder + PENALTY * code_totals[:, None] * decoder_wide / dec_norm[:, None]
    grad_enc_bias = jnp.sum(d_pre, axis=0)
    pre_totals = jnp.sum(d_pre_b.astype(jnp.float32), axis=0)
    bias_pull = jnp.dot(
        sae_encoder.astype(jnp.float32), pre_totals, precision=lax.Precision.HIGHEST
    )
    objective_part = jnp.sum(residual * residual) + PENALTY * jnp.sum(latent_codes * dec_norm)
    pull_total, objective = lax.psum((bias_pull, objective_part), ("expert", "dp"))
    grad_dec_bias = jnp.sum(d_recon.astype(jnp.float32), axis=0) - pull_total
    token_total = d_recon.shape[0]
    loss_mean = (objective / (token_total * d_recon.shape[1])).reshape(1)
    return (
        moe_out,
        grad_encoder.astype(jnp.bfloat16),
        grad_decoder.astype(jnp.bfloat16),
        grad_enc_bias,
        grad_dec_bias,
        loss_mean,
    )


ROWS = 16
NT = (((1,), (1,)), ((), ()))
F32 = jnp.float32
BF16 = jnp.bfloat16
MESH_IDS = pl.DeviceIdType.MESH


def mm(a, b):
    return jnp.dot(a, b, preferred_element_type=F32)


def layer_kernel(
    n_tok,
    n_chip,
    tok_hbm,
    routes_hbm,
    route_weights_hbm,
    w_gate,
    w_up,
    w_down,
    enc_hbm,
    enc_bias_hbm,
    dec_hbm,
    dec_bias_hbm,
    moe_hbm,
    g_enc_hbm,
    g_dec_hbm,
    g_enc_bias_hbm,
    g_dec_bias_hbm,
    loss_hbm,
    moe_out,
    g_enc,
    g_dec,
    g_enc_bias,
    g_dec_bias,
    loss,
    tokens,
    routes,
    route_weights,
    enc_bias,
    dec_bias,
    wg,
    wu,
    wd,
    enc,
    dec,
    tok_all,
    weight_all,
    part_send,
    part_recv,
    own_pre,
    hid_send,
    hid_recv,
    moe_sib_send,
    moe_sib_recv,
    moe_own,
    moe_z_send,
    moe_z_recv,
    moe_all,
    rec_sib_send,
    rec_sib_recv,
    rec_own,
    rec_dp_send,
    rec_dp_recv,
    rec_z_send,
    rec_z_recv,
    d_all,
    tot_send,
    tot_recv,
    centered_ref,
    load_sem,
    send_sem,
    tok_sem,
    weight_sem,
    pair_sem,
    moe_sem,
    moe_all_sem,
    rec_sem,
    d_all_sem,
    tot_sem,
    store_sem,
):
    expert = lax.axis_index("expert")
    p = lax.axis_index("dp")
    z, c = expert // 2, expert % 2
    q, s = 1 - p, 1 - c
    half = tokens.shape[1]
    width = 2 * half
    ff = wg.shape[2]
    tile = part_send.shape[-1]
    tiles = ff // tile
    rows = 2 * n_chip * ROWS
    side = n_chip * ROWS

    loads = []
    for slot, (hbm, vmem) in enumerate(
        (
            (tok_hbm, tokens),
            (routes_hbm, routes),
            (route_weights_hbm, route_weights),
            (w_gate.at[q], wg.at[0]),
            (w_up.at[q], wu.at[0]),
            (w_gate.at[p], wg.at[1]),
            (w_up.at[p], wu.at[1]),
            (w_down.at[p], wd.at[1]),
            (w_down.at[q], wd.at[0]),
            (dec_hbm, dec),
            (enc_hbm, enc),
            (enc_bias_hbm, enc_bias),
            (dec_bias_hbm, dec_bias),
        )
    ):
        load = pltpu.make_async_copy(hbm, vmem, load_sem.at[slot])
        load.start()
        loads.append(load)

    sibling = {"expert": z * 2 + s, "dp": p}
    across = {"expert": expert, "dp": q}
    chips = [{"expert": lax.rem(z + d, n_chip) * 2 + c, "dp": p} for d in range(n_chip)]

    barrier = pltpu.get_barrier_semaphore()
    diagonal = {"expert": z * 2 + s, "dp": q}
    peers = [sibling, across, diagonal] + chips[1:]
    for peer in peers:
        pl.semaphore_signal(barrier, inc=1, device_id=peer, device_id_type=MESH_IDS)

    base = pl.multiple_of((c * n_chip + z) * ROWS, ROWS)
    loads[0].wait()
    block = jnp.concatenate(
        [tokens[...], jnp.zeros((ROWS - n_tok, half), BF16)], axis=0
    )
    tok_all[pl.ds(base, ROWS), :] = block
    loads[1].wait()
    loads[2].wait()
    wide = (128, 128)
    fill = jnp.zeros((routes.shape[0], 128 - n_tok), jnp.int32)
    named = jnp.concatenate([routes[...], fill], axis=1)
    given = jnp.concatenate([route_weights[...], fill.astype(F32)], axis=1)
    of_expert = lax.broadcasted_iota(jnp.int32, wide, 0)
    dense = jnp.zeros(wide, F32)
    for k in range(routes.shape[0]):
        dense += jnp.where(of_expert == named[k : k + 1, :], given[k : k + 1, :], 0.0)
    weight_all[pl.ds(base, ROWS), :] = dense.T[:ROWS, :]
    pl.semaphore_wait(barrier, len(peers))

    pending = []
    stores = []

    def store(vmem, hbm):
        copy = pltpu.make_async_copy(vmem, hbm, store_sem.at[len(stores)])
        copy.start()
        stores.append(copy)

    def send(src, dst, recv, device):
        copy = pltpu.make_async_remote_copy(
            src_ref=src,
            dst_ref=dst,
            send_sem=send_sem.at[len(pending)],
            recv_sem=recv,
            device_id=device,
            device_id_type=MESH_IDS,
        )
        copy.start()
        pending.append(copy)

    def arrived(dst, recv):
        pltpu.make_async_remote_copy(
            src_ref=dst,
            dst_ref=dst,
            send_sem=send_sem.at[0],
            recv_sem=recv,
            device_id=across,
            device_id_type=MESH_IDS,
        ).wait_recv()

    def row_of(zz, cc):
        return pl.multiple_of((cc * n_chip + zz) * ROWS, ROWS)

    near = [lax.rem(z - d + n_chip, n_chip) for d in range(n_chip)]

    def rows_block(ref, zz, cc):
        return ref.at[pl.ds(row_of(zz, cc), ROWS), :]

    def gather_rows(pairs):
        for d in range(1, n_chip):
            for ref, sem in pairs:
                blk = rows_block(ref, z, c)
                send(blk, blk, sem.at[c * n_chip + z], chips[d])
        for d in range(n_chip):
            for ref, sem in pairs:
                blk = rows_block(ref, near[d], c)
                at = sem.at[c * n_chip + near[d]]
                if d:
                    arrived(blk, at)
                send(blk, blk, at, sibling)

    def finish_rows(ref, sem):
        for d in range(n_chip):
            arrived(rows_block(ref, near[d], s), sem.at[s * n_chip + near[d]])

    gather_rows([(tok_all, tok_sem), (weight_all, weight_sem)])

    loads[9].wait()
    squares = dec[...].astype(F32)
    norm_col = jnp.sqrt(jnp.sum(squares * squares, axis=1, keepdims=True) + EPSILON)
    latents = norm_col.shape[0]
    norm_rows = jnp.broadcast_to(norm_col, (latents, 128)).T
    norm_row = norm_rows[0:1, :]

    finish_rows(tok_all, tok_sem)

    loads[3].wait()
    loads[4].wait()
    for t in range(tiles):
        cols = slice(t * tile, (t + 1) * tile)
        for which, weights in enumerate((wg, wu)):
            part_send[t, which] = mm(tok_all[...], weights[0, :, cols]).astype(BF16)
        send(part_send.at[t], part_recv.at[t], pair_sem.at[t], across)
    loads[5].wait()
    loads[6].wait()
    for t in range(tiles):
        cols = slice(t * tile, (t + 1) * tile)
        for which, weights in enumerate((wg, wu)):
            own_pre[t, which] = mm(tok_all[...], weights[1, :, cols])

    finish_rows(weight_all, weight_sem)
    lane_all = lax.broadcasted_iota(jnp.int32, (rows, 128), 1)

    def share_of(index):
        return jnp.sum(
            jnp.where(lane_all == expert * 2 + index, weight_all[...], 0.0), axis=1, keepdims=True
        )

    share_own, share_other = share_of(p), share_of(q)
    for t in range(tiles):
        arrived(part_recv.at[t], pair_sem.at[t])
        gate = own_pre[t, 0] + part_recv[t, 0].astype(F32)
        up = own_pre[t, 1] + part_recv[t, 1].astype(F32)
        hid_send[t] = (gate / (1.0 + jnp.exp(-gate)) * up).astype(BF16)
        send(hid_send.at[t], hid_recv.at[t], pair_sem.at[tiles + t], across)

    sib_at = pl.multiple_of(s * side, side)
    loads[7].wait()
    loads[8].wait()
    down = mm(hid_send[0], wd[1, :tile])
    for t in range(1, tiles):
        down += mm(hid_send[t], wd[1, t * tile : (t + 1) * tile])
    moe_own[...] = share_own * down
    for t in range(tiles):
        arrived(hid_recv.at[t], pair_sem.at[tiles + t])
        moe_own[...] += share_other * mm(hid_recv[t], wd[0, t * tile : (t + 1) * tile])

    moe_sib_send[...] = moe_own[pl.ds(sib_at, side), :].astype(BF16)
    send(moe_sib_send, moe_sib_recv, moe_sem.at[n_chip], sibling)
    arrived(moe_sib_recv, moe_sem.at[n_chip])
    for d in list(range(1, n_chip)) + [0]:
        zz = lax.rem(z + d, n_chip)
        own_rows = pl.ds(pl.multiple_of(zz * ROWS, ROWS), ROWS)
        total = moe_own[pl.ds(row_of(zz, c), ROWS), :] + moe_sib_recv[own_rows, :].astype(F32)
        if d:
            moe_z_send[d] = total.astype(BF16)
            send(moe_z_send.at[d], moe_z_recv.at[d], moe_sem.at[d], chips[d])
    for d in range(1, n_chip):
        arrived(moe_z_recv.at[d], moe_sem.at[d])
        total += moe_z_recv[d].astype(F32)
    moe_block = total.astype(BF16)
    moe_out[...] = moe_block[:n_tok]
    store(moe_out, moe_hbm)
    own_cols = pl.ds(pl.multiple_of(p * half, half), half)
    other_cols = pl.ds(pl.multiple_of(q * half, half), half)
    moe_all[pl.ds(base, ROWS), own_cols] = moe_block

    def gather_all(ref, sem):
        def blk(zz, cc, cols):
            return ref.at[pl.ds(row_of(zz, cc), ROWS), cols]

        def at(zz, cc, pp):
            return sem.at[(cc * n_chip + zz) * 2 + pp]

        for d in range(1, n_chip):
            send(blk(z, c, own_cols), blk(z, c, own_cols), at(z, c, p), chips[d])
        for zz in near:
            if zz is not near[0]:
                arrived(blk(zz, c, own_cols), at(zz, c, p))
            send(blk(zz, c, own_cols), blk(zz, c, own_cols), at(zz, c, p), across)
            send(blk(zz, c, own_cols), blk(zz, c, own_cols), at(zz, c, p), sibling)
        for zz in near:
            arrived(blk(zz, c, other_cols), at(zz, c, q))
            send(blk(zz, c, other_cols), blk(zz, c, other_cols), at(zz, c, q), sibling)
        for zz in near:
            arrived(blk(zz, s, own_cols), at(zz, s, p))
            arrived(blk(zz, s, other_cols), at(zz, s, q))

    gather_all(moe_all, moe_all_sem)
    for slot in (10, 11, 12):
        loads[slot].wait()
    centered = (moe_all[...].astype(F32) - dec_bias[...]).astype(BF16)
    pre_act = lax.dot_general(centered, enc[...], NT, preferred_element_type=F32) + enc_bias[...]
    real = lax.broadcasted_iota(jnp.int32, (rows, 1), 0) % ROWS < n_tok
    scaled = SHARPNESS * pre_act
    codes = (jnp.maximum(scaled, 0.0) + jnp.log1p(jnp.exp(-jnp.abs(scaled)))) / SHARPNESS
    codes = jnp.where(real, codes, 0.0)
    codes_b = codes.astype(BF16)

    rec_own[...] = mm(codes_b, dec[...])
    rec_sib_send[...] = rec_own[pl.ds(sib_at, side), :].astype(BF16)
    send(rec_sib_send, rec_sib_recv, rec_sem.at[0], sibling)
    gates = 1.0 / (1.0 + jnp.exp(-scaled))
    gates = jnp.where(real, gates, 0.0)
    arrived(rec_sib_recv, rec_sem.at[0])
    order = list(range(1, n_chip)) + [0]
    kept = []
    for d in order:
        zz = lax.rem(z + d, n_chip)
        here = pl.ds(pl.multiple_of(zz * ROWS, ROWS), ROWS)
        there = pl.ds(row_of(zz, c), ROWS)
        rec_dp_send[d] = (
            rec_own[there, other_cols] + rec_sib_recv[here, other_cols].astype(F32)
        ).astype(BF16)
        send(rec_dp_send.at[d], rec_dp_recv.at[d], rec_sem.at[1 + d], across)
        kept.append(rec_own[there, own_cols] + rec_sib_recv[here, own_cols].astype(F32))
    for d, part in zip(order, kept):
        arrived(rec_dp_recv.at[d], rec_sem.at[1 + d])
        recon = part + rec_dp_recv[d].astype(F32)
        if d:
            rec_z_send[d] = recon.astype(BF16)
            send(rec_z_send.at[d], rec_z_recv.at[d], rec_sem.at[1 + n_chip + d], chips[d])
    centered_ref[...] = centered
    codes_t = codes.T
    code_totals = jnp.sum(codes_t, axis=1, keepdims=True)
    codes_bt = codes_t.astype(BF16)
    pull_scale = PENALTY * code_totals / norm_col
    for d in range(1, n_chip):
        arrived(rec_z_recv.at[d], rec_sem.at[1 + n_chip + d])
        recon += rec_z_recv[d].astype(F32)
    residual = recon + dec_bias[:, own_cols] - moe_all[pl.ds(base, ROWS), own_cols].astype(F32)
    mine = lax.broadcasted_iota(jnp.int32, (ROWS, 1), 0) < n_tok
    residual = jnp.where(mine, residual, 0.0)
    d_all[pl.ds(base, ROWS), own_cols] = (2.0 * residual).astype(BF16)
    objective = jnp.sum(residual * residual) + PENALTY * jnp.sum(codes * norm_row)
    gather_all(d_all, d_all_sem)

    d_recon = d_all[...]
    grad_codes = lax.dot_general(d_recon, dec[...], NT, preferred_element_type=F32)
    d_pre = (grad_codes + PENALTY * norm_row) * gates
    d_pre_b = d_pre.astype(BF16)
    g_enc_bias[...] = jnp.sum(d_pre, axis=0, keepdims=True)
    store(g_enc_bias, g_enc_bias_hbm)
    totals = jnp.sum(d_pre_b.astype(F32), axis=0, keepdims=True)
    high = totals.astype(BF16)
    rest = totals - high.astype(F32)
    mid = rest.astype(BF16)
    low = (rest - mid.astype(F32)).astype(BF16)
    thirds = jnp.concatenate(
        [high, mid, low, jnp.zeros((ROWS - 3, latents), BF16)], axis=0
    )
    pulls = mm(thirds, enc[...])
    tot_send[0, :, :width] = jnp.sum(pulls, axis=0, keepdims=True)
    tot_send[0, :, width:] = jnp.full((1, 128), objective, F32)

    for slot, device in enumerate((sibling, across, diagonal)):
        send(tot_send.at[0], tot_recv.at[slot], tot_sem.at[slot], device)
    d_pre_t = d_pre.T.astype(BF16)
    g_enc[...] = mm(d_pre_t, centered_ref[...]).astype(BF16)
    store(g_enc, g_enc_hbm)
    total = tot_send[0]
    for slot in range(3):
        arrived(tot_recv.at[slot], tot_sem.at[slot])
        total = total + tot_recv[slot]
    tot_send[1] = total
    for d in range(1, n_chip):
        send(tot_send.at[1], tot_recv.at[2 + d], tot_sem.at[2 + d], chips[d])
    g_dec[...] = (mm(codes_bt, d_recon) + pull_scale * dec[...].astype(F32)).astype(BF16)
    store(g_dec, g_dec_hbm)
    d_sum = jnp.sum(d_recon.astype(F32), axis=0, keepdims=True)
    final = total
    for d in range(1, n_chip):
        arrived(tot_recv.at[2 + d], tot_sem.at[2 + d])
        final = final + tot_recv[2 + d]
    g_dec_bias[...] = d_sum - final[:, :width]
    loss[...] = final[:, width:] / (n_tok * 2 * n_chip * width)
    store(g_dec_bias, g_dec_bias_hbm)
    store(loss, loss_hbm)
    for copy in pending:
        copy.wait_send()
    for copy in stores:
        copy.wait()


def hand_over(count, *refs):
    held = refs[2 * count : 3 * count]
    sems = refs[-1]
    reads = [pltpu.make_async_copy(refs[i], held[i], sems.at[i]) for i in range(count)]
    writes = [
        pltpu.make_async_copy(held[i], refs[count + i], sems.at[count + i]) for i in range(count)
    ]
    for copy in reads:
        copy.start()
    for read, write in zip(reads, writes):
        read.wait()
        write.start()
    for copy in writes:
        copy.wait()


def local_fused(
    tokens,
    routes,
    route_weights,
    w_gate,
    w_up,
    w_down,
    sae_encoder,
    enc_bias,
    sae_decoder,
    dec_bias,
):
    n_tok, half = tokens.shape
    n_chip = lax.axis_size("expert") // 2
    width = 2 * half
    ff = w_gate.shape[2]
    latents = enc_bias.shape[0]
    side = n_chip * ROWS
    rows = 2 * side
    tile = 256 if ff % 256 == 0 else ff
    tiles = ff // tile
    top = routes.shape[1]
    hbm = pl.BlockSpec(memory_space=pltpu.HBM)
    dma = pltpu.SemaphoreType.DMA
    shapes = (
        jax.ShapeDtypeStruct((n_tok, half), BF16),
        jax.ShapeDtypeStruct((latents, width), BF16),
        jax.ShapeDtypeStruct((latents, width), BF16),
        jax.ShapeDtypeStruct((1, latents), F32),
        jax.ShapeDtypeStruct((1, width), F32),
        jax.ShapeDtypeStruct((1, 128), F32),
    )
    scratch = [pltpu.VMEM(out.shape, out.dtype) for out in shapes] + [
        pltpu.VMEM((n_tok, half), BF16),
        pltpu.VMEM((top, n_tok), jnp.int32),
        pltpu.VMEM((top, n_tok), F32),
        pltpu.VMEM((1, latents), F32),
        pltpu.VMEM((1, width), F32),
        pltpu.VMEM((2, half, ff), BF16),
        pltpu.VMEM((2, half, ff), BF16),
        pltpu.VMEM((2, ff, half), BF16),
        pltpu.VMEM((latents, width), BF16),
        pltpu.VMEM((latents, width), BF16),
        pltpu.VMEM((rows, half), BF16),
        pltpu.VMEM((rows, 128), F32),
        pltpu.VMEM((tiles, 2, rows, tile), BF16),
        pltpu.VMEM((tiles, 2, rows, tile), BF16),
        pltpu.VMEM((tiles, 2, rows, tile), F32),
        pltpu.VMEM((tiles, rows, tile), BF16),
        pltpu.VMEM((tiles, rows, tile), BF16),
        pltpu.VMEM((side, half), BF16),
        pltpu.VMEM((side, half), BF16),
        pltpu.VMEM((rows, half), F32),
        pltpu.VMEM((n_chip, ROWS, half), BF16),
        pltpu.VMEM((n_chip, ROWS, half), BF16),
        pltpu.VMEM((rows, width), BF16),
        pltpu.VMEM((side, width), BF16),
        pltpu.VMEM((side, width), BF16),
        pltpu.VMEM((rows, width), F32),
        pltpu.VMEM((n_chip, ROWS, half), BF16),
        pltpu.VMEM((n_chip, ROWS, half), BF16),
        pltpu.VMEM((n_chip, ROWS, half), BF16),
        pltpu.VMEM((n_chip, ROWS, half), BF16),
        pltpu.VMEM((rows, width), BF16),
        pltpu.VMEM((2, 1, width + 128), F32),
        pltpu.VMEM((2 + n_chip, 1, width + 128), F32),
        pltpu.VMEM((rows, width), BF16),
        dma((13,)),
        dma((16 * n_chip + 2 * tiles,)),
        dma((2 * n_chip,)),
        dma((2 * n_chip,)),
        dma((2 * tiles,)),
        dma((n_chip + 1,)),
        dma((4 * n_chip,)),
        dma((1 + 2 * n_chip,)),
        dma((4 * n_chip,)),
        dma((2 + n_chip,)),
        dma((len(shapes),)),
    ]
    outs = pl.pallas_call(
        functools.partial(layer_kernel, n_tok, n_chip),
        out_shape=shapes,
        in_specs=[hbm] * 10,
        out_specs=(hbm,) * 6,
        scratch_shapes=scratch,
        compiler_params=pltpu.CompilerParams(
            collective_id=0, has_side_effects=True, vmem_limit_bytes=63 * 1024 * 1024
        ),
    )(
        tokens,
        routes.T,
        route_weights.T,
        w_gate,
        w_up,
        w_down,
        sae_encoder.T,
        enc_bias.reshape(1, -1),
        sae_decoder,
        dec_bias.reshape(1, -1),
    )
    moe_out, g_enc, g_dec, g_enc_bias, g_dec_bias, loss = pl.pallas_call(
        functools.partial(hand_over, len(shapes)),
        out_shape=shapes,
        in_specs=[hbm] * len(shapes),
        out_specs=(hbm,) * len(shapes),
        scratch_shapes=[pltpu.VMEM(out.shape, out.dtype) for out in shapes]
        + [dma((2 * len(shapes),))],
        compiler_params=pltpu.CompilerParams(vmem_limit_bytes=63 * 1024 * 1024),
    )(*outs)
    return moe_out, g_enc.T, g_dec, g_enc_bias.reshape(-1), g_dec_bias.reshape(-1), loss[0, :1]


def local(*args):
    tokens, w_gate = args[0], args[3]
    pairs = lax.axis_size("dp") == 2 and w_gate.shape[0] == 2
    total_experts = 2 * lax.axis_size("expert")
    if pairs and lax.axis_size("expert") % 2 == 0 and total_experts <= 32 and tokens.shape[0] <= ROWS:
        return local_fused(*args)
    return local_plain(*args)


def solution(mesh):
    in_specs = (
        P(("groups", "expert"), "dp"),
        P(("groups", "expert"), None),
        P(("groups", "expert"), None),
        P("expert", "dp", None),
        P("expert", "dp", None),
        P("expert", None, "dp"),
        P(None, ("expert", "dp")),
        P(("expert", "dp")),
        P(("expert", "dp"), None),
        P(),
    )
    out_specs = (
        P(("groups", "expert"), "dp"),
        P("groups", ("expert", "dp")),
        P(("expert", "dp"), "groups"),
        P(("groups", "expert", "dp")),
        P("groups"),
        P("groups"),
    )
    return jax.shard_map(local, mesh=mesh, in_specs=in_specs, out_specs=out_specs, check_vma=False)
```

```python
import functools

import jax
import jax.numpy as jnp
from jax import lax
from jax.experimental import pallas as pl
from jax.experimental.pallas import tpu as pltpu
from jax.sharding import PartitionSpec as P

PENALTY = 0.5
SHARPNESS = 4.0
EPSILON = 1e-06


def gather_tokens(local_block):
    widened = lax.all_gather(local_block, "dp", axis=1, tiled=True)
    return lax.all_gather(widened, "expert", axis=0, tiled=True)


def local_plain(
    tokens,
    routes,
    route_weights,
    w_gate,
    w_up,
    w_down,
    sae_encoder,
    enc_bias,
    sae_decoder,
    dec_bias,
):
    tok_count, top_count = routes.shape
    feature_width = tokens.shape[1]
    local_experts = w_gate.shape[0]
    peer_count = lax.axis_size("expert")
    total_experts = local_experts * peer_count
    capacity = min(tok_count, max(2, tok_count * top_count * 3 // (2 * total_experts)))
    flat_routes = routes.reshape(-1)
    expert_hot = (
        flat_routes[:, None] == jnp.arange(total_experts, dtype=jnp.int32)[None, :]
    ).astype(jnp.int32)
    earlier = jnp.cumsum(expert_hot, axis=0) - expert_hot
    position = jnp.sum(earlier * expert_hot, axis=1)
    slot_index = flat_routes * capacity + position
    slot_hot = slot_index[:, None] == jnp.arange(total_experts * capacity, dtype=jnp.int32)[None, :]
    slot_hot = slot_hot.reshape(tok_count, top_count, total_experts * capacity)
    dispatch_map = jnp.sum(slot_hot.astype(jnp.int32), axis=1).astype(jnp.bfloat16)
    combine_map = jnp.sum(slot_hot.astype(jnp.float32) * route_weights[:, :, None], axis=1)
    send_rows = lax.dot_general(
        dispatch_map, tokens, (((0,), (0,)), ((), ())), preferred_element_type=jnp.float32
    )
    send_blocks = send_rows.astype(jnp.bfloat16).reshape(
        peer_count, local_experts, capacity, feature_width
    )
    received = lax.all_to_all(send_blocks, "expert", split_axis=0, concat_axis=0, tiled=True)
    gate_part = jnp.einsum("secd,edf->secf", received, w_gate, preferred_element_type=jnp.float32)
    up_part = jnp.einsum("secd,edf->secf", received, w_up, preferred_element_type=jnp.float32)
    gate_full, up_full = lax.psum((gate_part, up_part), "dp")
    hidden = (jax.nn.silu(gate_full) * up_full).astype(jnp.bfloat16)
    outputs = jnp.einsum("secf,efd->secd", hidden, w_down, preferred_element_type=jnp.float32)
    returned = lax.all_to_all(
        outputs.astype(jnp.bfloat16), "expert", split_axis=0, concat_axis=0, tiled=True
    )
    returned_rows = returned.reshape(total_experts * capacity, feature_width).astype(jnp.float32)
    combined = jnp.dot(combine_map, returned_rows, precision=lax.Precision.HIGHEST)
    moe_out = combined.astype(jnp.bfloat16)
    all_tokens = gather_tokens(moe_out)
    centered = (all_tokens.astype(jnp.float32) - dec_bias).astype(jnp.bfloat16)
    pre_act = jnp.dot(centered, sae_encoder, preferred_element_type=jnp.float32) + enc_bias
    latent_codes = jax.nn.softplus(SHARPNESS * pre_act) / SHARPNESS
    codes_b = latent_codes.astype(jnp.bfloat16)
    decoder_wide = sae_decoder.astype(jnp.float32)
    dec_norm = jnp.sqrt(jnp.sum(decoder_wide * decoder_wide, axis=1) + EPSILON)
    partial_rows = lax.psum_scatter(
        jnp.dot(codes_b, sae_decoder, preferred_element_type=jnp.float32).astype(jnp.bfloat16),
        "expert",
        scatter_dimension=0,
        tiled=True,
    )
    recon_share = lax.psum_scatter(partial_rows, "dp", scatter_dimension=1, tiled=True).astype(
        jnp.float32
    )
    bias_share = lax.dynamic_slice_in_dim(
        dec_bias, lax.axis_index("dp") * feature_width, feature_width, 0
    )
    residual = recon_share + bias_share - moe_out.astype(jnp.float32)
    d_recon_share = (2.0 * residual).astype(jnp.bfloat16)
    d_recon = gather_tokens(d_recon_share)
    grad_codes = lax.dot_general(
        d_recon, sae_decoder, (((1,), (1,)), ((), ())), preferred_element_type=jnp.float32
    )
    d_pre = (grad_codes + PENALTY * dec_norm) * jax.nn.sigmoid(SHARPNESS * pre_act)
    d_pre_b = d_pre.astype(jnp.bfloat16)
    grad_encoder = lax.dot_general(
        centered, d_pre_b, (((0,), (0,)), ((), ())), preferred_element_type=jnp.float32
    )
    code_totals = jnp.sum(latent_codes, axis=0)
    grad_decoder = lax.dot_general(
        codes_b, d_recon, (((0,), (0,)), ((), ())), preferred_element_type=jnp.float32
    )
    grad_decoder = grad_decoder + PENALTY * code_totals[:, None] * decoder_wide / dec_norm[:, None]
    grad_enc_bias = jnp.sum(d_pre, axis=0)
    pre_totals = jnp.sum(d_pre_b.astype(jnp.float32), axis=0)
    bias_pull = jnp.dot(
        sae_encoder.astype(jnp.float32), pre_totals, precision=lax.Precision.HIGHEST
    )
    objective_part = jnp.sum(residual * residual) + PENALTY * jnp.sum(latent_codes * dec_norm)
    pull_total, objective = lax.psum((bias_pull, objective_part), ("expert", "dp"))
    grad_dec_bias = jnp.sum(d_recon.astype(jnp.float32), axis=0) - pull_total
    token_total = d_recon.shape[0]
    loss_mean = (objective / (token_total * d_recon.shape[1])).reshape(1)
    return (
        moe_out,
        grad_encoder.astype(jnp.bfloat16),
        grad_decoder.astype(jnp.bfloat16),
        grad_enc_bias,
        grad_dec_bias,
        loss_mean,
    )


ROWS = 16
NT = (((1,), (1,)), ((), ()))
F32 = jnp.float32
BF16 = jnp.bfloat16
MESH_IDS = pl.DeviceIdType.MESH


def mm(a, b):
    return jnp.dot(a, b, preferred_element_type=F32)


def layer_kernel(
    n_tok,
    n_chip,
    tok_hbm,
    routes_hbm,
    route_weights_hbm,
    w_gate,
    w_up,
    w_down,
    enc_hbm,
    enc_bias_hbm,
    dec_hbm,
    dec_bias_hbm,
    moe_hbm,
    g_enc_hbm,
    g_dec_hbm,
    g_enc_bias_hbm,
    g_dec_bias_hbm,
    loss_hbm,
    moe_out,
    g_enc,
    g_dec,
    g_enc_bias,
    g_dec_bias,
    loss,
    tokens,
    routes,
    route_weights,
    enc_bias,
    dec_bias,
    wg,
    wu,
    wd,
    enc,
    dec,
    tok_all,
    weight_all,
    picked,
    part_send,
    part_recv,
    own_pre,
    hid_send,
    hid_recv,
    moe_sib_send,
    moe_sib_recv,
    moe_own,
    moe_z_send,
    moe_z_recv,
    moe_all,
    rec_sib_send,
    rec_sib_recv,
    rec_own,
    rec_dp_send,
    rec_dp_recv,
    rec_z_send,
    rec_z_recv,
    d_all,
    tot_send,
    tot_recv,
    centered_ref,
    load_sem,
    send_sem,
    tok_sem,
    weight_sem,
    pair_sem,
    moe_sem,
    moe_all_sem,
    rec_sem,
    d_all_sem,
    tot_sem,
    store_sem,
):
    expert = lax.axis_index("expert")
    p = lax.axis_index("dp")
    z, c = expert // 2, expert % 2
    q, s = 1 - p, 1 - c
    half = tokens.shape[1]
    width = 2 * half
    ff = wg.shape[2]
    tile = part_send.shape[-1]
    tiles = ff // tile
    rows = 2 * n_chip * ROWS
    side = n_chip * ROWS

    loads = []
    for slot, (hbm, vmem) in enumerate(
        (
            (tok_hbm, tokens),
            (routes_hbm, routes),
            (route_weights_hbm, route_weights),
            (w_gate.at[q], wg.at[0]),
            (w_up.at[q], wu.at[0]),
            (w_gate.at[p], wg.at[1]),
            (w_up.at[p], wu.at[1]),
            (w_down.at[p], wd.at[1]),
            (w_down.at[q], wd.at[0]),
            (dec_hbm, dec),
            (enc_hbm, enc),
            (enc_bias_hbm, enc_bias),
            (dec_bias_hbm, dec_bias),
        )
    ):
        load = pltpu.make_async_copy(hbm, vmem, load_sem.at[slot])
        load.start()
        loads.append(load)

    sibling = {"expert": z * 2 + s, "dp": p}
    across = {"expert": expert, "dp": q}
    chips = [{"expert": lax.rem(z + d, n_chip) * 2 + c, "dp": p} for d in range(n_chip)]

    barrier = pltpu.get_barrier_semaphore()
    diagonal = {"expert": z * 2 + s, "dp": q}
    peers = [sibling, across, diagonal] + chips[1:]
    for peer in peers:
        pl.semaphore_signal(barrier, inc=1, device_id=peer, device_id_type=MESH_IDS)

    base = pl.multiple_of((c * n_chip + z) * ROWS, ROWS)
    loads[0].wait()
    block = jnp.concatenate(
        [tokens[...], jnp.zeros((ROWS - n_tok, half), BF16)], axis=0
    )
    tok_all[pl.ds(base, ROWS), :] = block
    loads[1].wait()
    loads[2].wait()
    wide = (128, 128)
    fill = jnp.zeros((routes.shape[0], 128 - n_tok), jnp.int32)
    named = jnp.concatenate([routes[...], fill], axis=1)
    given = jnp.concatenate([route_weights[...], fill.astype(F32)], axis=1)
    of_expert = lax.broadcasted_iota(jnp.int32, wide, 0)
    dense = jnp.zeros(wide, F32)
    for k in range(routes.shape[0]):
        dense += jnp.where(of_expert == named[k : k + 1, :], given[k : k + 1, :], 0.0)
    weight_all[pl.ds(base, ROWS), :] = dense.T[:ROWS, :]
    pl.semaphore_wait(barrier, len(peers))

    pending = []
    stores = []

    def store(vmem, hbm):
        copy = pltpu.make_async_copy(vmem, hbm, store_sem.at[len(stores)])
        copy.start()
        stores.append(copy)

    def send(src, dst, recv, device):
        copy = pltpu.make_async_remote_copy(
            src_ref=src,
            dst_ref=dst,
            send_sem=send_sem.at[len(pending)],
            recv_sem=recv,
            device_id=device,
            device_id_type=MESH_IDS,
        )
        copy.start()
        pending.append(copy)

    def arrived(dst, recv):
        pltpu.make_async_remote_copy(
            src_ref=dst,
            dst_ref=dst,
            send_sem=send_sem.at[0],
            recv_sem=recv,
            device_id=across,
            device_id_type=MESH_IDS,
        ).wait_recv()

    def row_of(zz, cc):
        return pl.multiple_of((cc * n_chip + zz) * ROWS, ROWS)

    near = [lax.rem(z - d + n_chip, n_chip) for d in range(n_chip)]

    def rows_block(ref, zz, cc):
        return ref.at[pl.ds(row_of(zz, cc), ROWS), :]

    def gather_rows(pairs):
        for d in range(1, n_chip):
            for ref, sem in pairs:
                blk = rows_block(ref, z, c)
                send(blk, blk, sem.at[c * n_chip + z], chips[d])
        for d in range(n_chip):
            for ref, sem in pairs:
                blk = rows_block(ref, near[d], c)
                at = sem.at[c * n_chip + near[d]]
                if d:
                    arrived(blk, at)
                send(blk, blk, at, sibling)

    def finish_rows(ref, sem):
        for d in range(n_chip):
            arrived(rows_block(ref, near[d], s), sem.at[s * n_chip + near[d]])

    gather_rows([(tok_all, tok_sem), (weight_all, weight_sem)])

    loads[9].wait()
    squares = dec[...].astype(F32)
    norm_col = jnp.sqrt(jnp.sum(squares * squares, axis=1, keepdims=True) + EPSILON)
    latents = norm_col.shape[0]
    norm_rows = jnp.broadcast_to(norm_col, (latents, 128)).T
    norm_row = norm_rows[0:1, :]

    finish_rows(weight_all, weight_sem)
    slots = picked.shape[1]
    by_expert = weight_all[...].T
    of_row = lax.broadcasted_iota(jnp.int32, by_expert.shape, 0)
    lane_all = lax.broadcasted_iota(jnp.int32, (rows, 128), 1)
    before = lax.broadcasted_iota(jnp.int32, (rows, rows), 0)
    before = (before < lax.broadcasted_iota(jnp.int32, (rows, rows), 1)).astype(BF16)
    slot_of = lax.broadcasted_iota(jnp.int32, (slots, rows), 0).astype(F32)
    shares, hots = [], []
    for index in (q, p):
        number = expert * 2 + index
        given_row = jnp.sum(jnp.where(of_row == number, by_expert, 0.0), axis=0, keepdims=True)
        named_row = jnp.where(given_row > 0.0, 1.0, 0.0)
        place = mm(jnp.broadcast_to(named_row, (ROWS, rows)).astype(BF16), before)[0:1, :]
        place = jnp.where(given_row > 0.0, place, -1.0)
        hots.append(jnp.where(slot_of == place, 1.0, 0.0))
        shares.append(
            jnp.sum(jnp.where(lane_all == number, weight_all[...], 0.0), axis=1, keepdims=True)
        )
    share_other, share_own = shares
    back_other, back_own = [hot.T.astype(BF16) for hot in hots]
    finish_rows(tok_all, tok_sem)
    picked[0] = mm(hots[0].astype(BF16), tok_all[...]).astype(BF16)

    loads[3].wait()
    loads[4].wait()
    for t in range(tiles):
        cols = slice(t * tile, (t + 1) * tile)
        for which, weights in enumerate((wg, wu)):
            part_send[t, which] = mm(picked[0], weights[0, :, cols]).astype(BF16)
        send(part_send.at[t], part_recv.at[t], pair_sem.at[t], across)
    picked[1] = mm(hots[1].astype(BF16), tok_all[...]).astype(BF16)
    loads[5].wait()
    loads[6].wait()
    for t in range(tiles):
        cols = slice(t * tile, (t + 1) * tile)
        for which, weights in enumerate((wg, wu)):
            own_pre[t, which] = mm(picked[1], weights[1, :, cols])

    for t in range(tiles):
        arrived(part_recv.at[t], pair_sem.at[t])
        gate = own_pre[t, 0] + part_recv[t, 0].astype(F32)
        up = own_pre[t, 1] + part_recv[t, 1].astype(F32)
        hid_send[t] = (gate / (1.0 + jnp.exp(-gate)) * up).astype(BF16)
        send(hid_send.at[t], hid_recv.at[t], pair_sem.at[tiles + t], across)

    sib_at = pl.multiple_of(s * side, side)
    loads[7].wait()
    loads[8].wait()
    down = mm(hid_send[0], wd[1, :tile])
    for t in range(1, tiles):
        down += mm(hid_send[t], wd[1, t * tile : (t + 1) * tile])
    moe_own[...] = share_own * mm(back_own, down.astype(BF16))
    arrived(hid_recv.at[0], pair_sem.at[tiles])
    down = mm(hid_recv[0], wd[0, :tile])
    for t in range(1, tiles):
        arrived(hid_recv.at[t], pair_sem.at[tiles + t])
        down += mm(hid_recv[t], wd[0, t * tile : (t + 1) * tile])
    moe_own[...] += share_other * mm(back_other, down.astype(BF16))

    moe_sib_send[...] = moe_own[pl.ds(sib_at, side), :].astype(BF16)
    send(moe_sib_send, moe_sib_recv, moe_sem.at[n_chip], sibling)
    arrived(moe_sib_recv, moe_sem.at[n_chip])
    for d in list(range(1, n_chip)) + [0]:
        zz = lax.rem(z + d, n_chip)
        own_rows = pl.ds(pl.multiple_of(zz * ROWS, ROWS), ROWS)
        total = moe_own[pl.ds(row_of(zz, c), ROWS), :] + moe_sib_recv[own_rows, :].astype(F32)
        if d:
            moe_z_send[d] = total.astype(BF16)
            send(moe_z_send.at[d], moe_z_recv.at[d], moe_sem.at[d], chips[d])
    for d in range(1, n_chip):
        arrived(moe_z_recv.at[d], moe_sem.at[d])
        total += moe_z_recv[d].astype(F32)
    moe_block = total.astype(BF16)
    moe_out[...] = moe_block[:n_tok]
    store(moe_out, moe_hbm)
    own_cols = pl.ds(pl.multiple_of(p * half, half), half)
    other_cols = pl.ds(pl.multiple_of(q * half, half), half)
    moe_all[pl.ds(base, ROWS), own_cols] = moe_block

    def gather_all(ref, sem):
        def blk(zz, cc, cols):
            return ref.at[pl.ds(row_of(zz, cc), ROWS), cols]

        def at(zz, cc, pp):
            return sem.at[(cc * n_chip + zz) * 2 + pp]

        for d in range(1, n_chip):
            send(blk(z, c, own_cols), blk(z, c, own_cols), at(z, c, p), chips[d])
        for zz in near:
            if zz is not near[0]:
                arrived(blk(zz, c, own_cols), at(zz, c, p))
            send(blk(zz, c, own_cols), blk(zz, c, own_cols), at(zz, c, p), across)
            send(blk(zz, c, own_cols), blk(zz, c, own_cols), at(zz, c, p), sibling)
        for zz in near:
            arrived(blk(zz, c, other_cols), at(zz, c, q))
            send(blk(zz, c, other_cols), blk(zz, c, other_cols), at(zz, c, q), sibling)
        for zz in near:
            arrived(blk(zz, s, own_cols), at(zz, s, p))
            arrived(blk(zz, s, other_cols), at(zz, s, q))

    gather_all(moe_all, moe_all_sem)
    for slot in (10, 11, 12):
        loads[slot].wait()
    centered = (moe_all[...].astype(F32) - dec_bias[...]).astype(BF16)
    pre_act = lax.dot_general(centered, enc[...], NT, preferred_element_type=F32) + enc_bias[...]
    real = lax.broadcasted_iota(jnp.int32, (rows, 1), 0) % ROWS < n_tok
    scaled = SHARPNESS * pre_act
    codes = (jnp.maximum(scaled, 0.0) + jnp.log1p(jnp.exp(-jnp.abs(scaled)))) / SHARPNESS
    codes = jnp.where(real, codes, 0.0)
    codes_b = codes.astype(BF16)

    rec_own[...] = mm(codes_b, dec[...])
    rec_sib_send[...] = rec_own[pl.ds(sib_at, side), :].astype(BF16)
    send(rec_sib_send, rec_sib_recv, rec_sem.at[0], sibling)
    gates = 1.0 / (1.0 + jnp.exp(-scaled))
    gates = jnp.where(real, gates, 0.0)
    arrived(rec_sib_recv, rec_sem.at[0])
    order = list(range(1, n_chip)) + [0]
    kept = []
    for d in order:
        zz = lax.rem(z + d, n_chip)
        here = pl.ds(pl.multiple_of(zz * ROWS, ROWS), ROWS)
        there = pl.ds(row_of(zz, c), ROWS)
        rec_dp_send[d] = (
            rec_own[there, other_cols] + rec_sib_recv[here, other_cols].astype(F32)
        ).astype(BF16)
        send(rec_dp_send.at[d], rec_dp_recv.at[d], rec_sem.at[1 + d], across)
        kept.append(rec_own[there, own_cols] + rec_sib_recv[here, own_cols].astype(F32))
    for d, part in zip(order, kept):
        arrived(rec_dp_recv.at[d], rec_sem.at[1 + d])
        recon = part + rec_dp_recv[d].astype(F32)
        if d:
            rec_z_send[d] = recon.astype(BF16)
            send(rec_z_send.at[d], rec_z_recv.at[d], rec_sem.at[1 + n_chip + d], chips[d])
    centered_ref[...] = centered
    codes_t = codes.T
    code_totals = jnp.sum(codes_t, axis=1, keepdims=True)
    codes_bt = codes_t.astype(BF16)
    pull_scale = PENALTY * code_totals / norm_col
    for d in range(1, n_chip):
        arrived(rec_z_recv.at[d], rec_sem.at[1 + n_chip + d])
        recon += rec_z_recv[d].astype(F32)
    residual = recon + dec_bias[:, own_cols] - moe_all[pl.ds(base, ROWS), own_cols].astype(F32)
    mine = lax.broadcasted_iota(jnp.int32, (ROWS, 1), 0) < n_tok
    residual = jnp.where(mine, residual, 0.0)
    d_all[pl.ds(base, ROWS), own_cols] = (2.0 * residual).astype(BF16)
    objective = jnp.sum(residual * residual) + PENALTY * jnp.sum(codes * norm_row)
    gather_all(d_all, d_all_sem)

    d_recon = d_all[...]
    grad_codes = lax.dot_general(d_recon, dec[...], NT, preferred_element_type=F32)
    d_pre = (grad_codes + PENALTY * norm_row) * gates
    d_pre_b = d_pre.astype(BF16)
    g_enc_bias[...] = jnp.sum(d_pre, axis=0, keepdims=True)
    store(g_enc_bias, g_enc_bias_hbm)
    totals = jnp.sum(d_pre_b.astype(F32), axis=0, keepdims=True)
    high = totals.astype(BF16)
    rest = totals - high.astype(F32)
    mid = rest.astype(BF16)
    low = (rest - mid.astype(F32)).astype(BF16)
    thirds = jnp.concatenate(
        [high, mid, low, jnp.zeros((ROWS - 3, latents), BF16)], axis=0
    )
    pulls = mm(thirds, enc[...])
    tot_send[0, :, :width] = jnp.sum(pulls, axis=0, keepdims=True)
    tot_send[0, :, width:] = jnp.full((1, 128), objective, F32)

    for slot, device in enumerate((sibling, across, diagonal)):
        send(tot_send.at[0], tot_recv.at[slot], tot_sem.at[slot], device)
    d_pre_t = d_pre.T.astype(BF16)
    g_enc[...] = mm(d_pre_t, centered_ref[...]).astype(BF16)
    store(g_enc, g_enc_hbm)
    total = tot_send[0]
    for slot in range(3):
        arrived(tot_recv.at[slot], tot_sem.at[slot])
        total = total + tot_recv[slot]
    tot_send[1] = total
    for d in range(1, n_chip):
        send(tot_send.at[1], tot_recv.at[2 + d], tot_sem.at[2 + d], chips[d])
    g_dec[...] = (mm(codes_bt, d_recon) + pull_scale * dec[...].astype(F32)).astype(BF16)
    store(g_dec, g_dec_hbm)
    d_sum = jnp.sum(d_recon.astype(F32), axis=0, keepdims=True)
    final = total
    for d in range(1, n_chip):
        arrived(tot_recv.at[2 + d], tot_sem.at[2 + d])
        final = final + tot_recv[2 + d]
    g_dec_bias[...] = d_sum - final[:, :width]
    loss[...] = final[:, width:] / (n_tok * 2 * n_chip * width)
    store(g_dec_bias, g_dec_bias_hbm)
    store(loss, loss_hbm)
    for copy in pending:
        copy.wait_send()
    for copy in stores:
        copy.wait()


def hand_over(count, *refs):
    held = refs[2 * count : 3 * count]
    sems = refs[-1]
    reads = [pltpu.make_async_copy(refs[i], held[i], sems.at[i]) for i in range(count)]
    writes = [
        pltpu.make_async_copy(held[i], refs[count + i], sems.at[count + i]) for i in range(count)
    ]
    for copy in reads:
        copy.start()
    for read, write in zip(reads, writes):
        read.wait()
        write.start()
    for copy in writes:
        copy.wait()


def local_fused(
    tokens,
    routes,
    route_weights,
    w_gate,
    w_up,
    w_down,
    sae_encoder,
    enc_bias,
    sae_decoder,
    dec_bias,
):
    n_tok, half = tokens.shape
    n_chip = lax.axis_size("expert") // 2
    width = 2 * half
    ff = w_gate.shape[2]
    latents = enc_bias.shape[0]
    side = n_chip * ROWS
    rows = 2 * side
    tile = 256 if ff % 256 == 0 else ff
    tiles = ff // tile
    top = routes.shape[1]
    peers = 2 * n_chip
    capacity = min(n_tok, max(2, n_tok * top * 3 // (4 * peers)))
    slots = -(-peers * capacity // ROWS) * ROWS
    hbm = pl.BlockSpec(memory_space=pltpu.HBM)
    dma = pltpu.SemaphoreType.DMA
    shapes = (
        jax.ShapeDtypeStruct((n_tok, half), BF16),
        jax.ShapeDtypeStruct((latents, width), BF16),
        jax.ShapeDtypeStruct((latents, width), BF16),
        jax.ShapeDtypeStruct((1, latents), F32),
        jax.ShapeDtypeStruct((1, width), F32),
        jax.ShapeDtypeStruct((1, 128), F32),
    )
    scratch = [pltpu.VMEM(out.shape, out.dtype) for out in shapes] + [
        pltpu.VMEM((n_tok, half), BF16),
        pltpu.VMEM((top, n_tok), jnp.int32),
        pltpu.VMEM((top, n_tok), F32),
        pltpu.VMEM((1, latents), F32),
        pltpu.VMEM((1, width), F32),
        pltpu.VMEM((2, half, ff), BF16),
        pltpu.VMEM((2, half, ff), BF16),
        pltpu.VMEM((2, ff, half), BF16),
        pltpu.VMEM((latents, width), BF16),
        pltpu.VMEM((latents, width), BF16),
        pltpu.VMEM((rows, half), BF16),
        pltpu.VMEM((rows, 128), F32),
        pltpu.VMEM((2, slots, half), BF16),
        pltpu.VMEM((tiles, 2, slots, tile), BF16),
        pltpu.VMEM((tiles, 2, slots, tile), BF16),
        pltpu.VMEM((tiles, 2, slots, tile), F32),
        pltpu.VMEM((tiles, slots, tile), BF16),
        pltpu.VMEM((tiles, slots, tile), BF16),
        pltpu.VMEM((side, half), BF16),
        pltpu.VMEM((side, half), BF16),
        pltpu.VMEM((rows, half), F32),
        pltpu.VMEM((n_chip, ROWS, half), BF16),
        pltpu.VMEM((n_chip, ROWS, half), BF16),
        pltpu.VMEM((rows, width), BF16),
        pltpu.VMEM((side, width), BF16),
        pltpu.VMEM((side, width), BF16),
        pltpu.VMEM((rows, width), F32),
        pltpu.VMEM((n_chip, ROWS, half), BF16),
        pltpu.VMEM((n_chip, ROWS, half), BF16),
        pltpu.VMEM((n_chip, ROWS, half), BF16),
        pltpu.VMEM((n_chip, ROWS, half), BF16),
        pltpu.VMEM((rows, width), BF16),
        pltpu.VMEM((2, 1, width + 128), F32),
        pltpu.VMEM((2 + n_chip, 1, width + 128), F32),
        pltpu.VMEM((rows, width), BF16),
        dma((13,)),
        dma((16 * n_chip + 2 * tiles,)),
        dma((2 * n_chip,)),
        dma((2 * n_chip,)),
        dma((2 * tiles,)),
        dma((n_chip + 1,)),
        dma((4 * n_chip,)),
        dma((1 + 2 * n_chip,)),
        dma((4 * n_chip,)),
        dma((2 + n_chip,)),
        dma((len(shapes),)),
    ]
    outs = pl.pallas_call(
        functools.partial(layer_kernel, n_tok, n_chip),
        out_shape=shapes,
        in_specs=[hbm] * 10,
        out_specs=(hbm,) * 6,
        scratch_shapes=scratch,
        compiler_params=pltpu.CompilerParams(
            collective_id=0, has_side_effects=True, vmem_limit_bytes=63 * 1024 * 1024
        ),
    )(
        tokens,
        routes.T,
        route_weights.T,
        w_gate,
        w_up,
        w_down,
        sae_encoder.T,
        enc_bias.reshape(1, -1),
        sae_decoder,
        dec_bias.reshape(1, -1),
    )
    moe_out, g_enc, g_dec, g_enc_bias, g_dec_bias, loss = pl.pallas_call(
        functools.partial(hand_over, len(shapes)),
        out_shape=shapes,
        in_specs=[hbm] * len(shapes),
        out_specs=(hbm,) * len(shapes),
        scratch_shapes=[pltpu.VMEM(out.shape, out.dtype) for out in shapes]
        + [dma((2 * len(shapes),))],
        compiler_params=pltpu.CompilerParams(vmem_limit_bytes=63 * 1024 * 1024),
    )(*outs)
    return moe_out, g_enc.T, g_dec, g_enc_bias.reshape(-1), g_dec_bias.reshape(-1), loss[0, :1]


def local(*args):
    tokens, w_gate = args[0], args[3]
    pairs = lax.axis_size("dp") == 2 and w_gate.shape[0] == 2
    total_experts = 2 * lax.axis_size("expert")
    if pairs and lax.axis_size("expert") % 2 == 0 and total_experts <= 32 and tokens.shape[0] <= ROWS:
        return local_fused(*args)
    return local_plain(*args)


def solution(mesh):
    in_specs = (
        P(("groups", "expert"), "dp"),
        P(("groups", "expert"), None),
        P(("groups", "expert"), None),
        P("expert", "dp", None),
        P("expert", "dp", None),
        P("expert", None, "dp"),
        P(None, ("expert", "dp")),
        P(("expert", "dp")),
        P(("expert", "dp"), None),
        P(),
    )
    out_specs = (
        P(("groups", "expert"), "dp"),
        P("groups", ("expert", "dp")),
        P(("expert", "dp"), "groups"),
        P(("groups", "expert", "dp")),
        P("groups"),
        P("groups"),
    )
    return jax.shard_map(local, mesh=mesh, in_specs=in_specs, out_specs=out_specs, check_vma=False)
```
